768 devices in a mesh: dp: 96 (over z, y), tensor: 8 (over x, core).
Axes of the slice: x: 4, y: 8, z: 12, core: 2. Of those that a mesh axis runs over, the one named last changes fastest.
Arguments:
- inputs: bfloat16 [49152, 5120], P('dp', 'tensor'), may hold values from -6 to 6
- cotangent: bfloat16 [49152, 1024], P('dp', 'tensor'), may hold values from -1.5 to 1.5
- base_weight: bfloat16 [5120, 1024], P('tensor'), may hold values from -0.078125 to 0.078125
- down_a: bfloat16 [192, 5120, 16], P('dp', 'tensor'), may hold values from -0.078125 to 0.078125
- up_b: bfloat16 [192, 16, 1024], P('dp', None, 'tensor'), may hold values from -1.5 to 1.5
- block_adapter: int32 [384], P('dp'), may hold values from 0 to 191, as said below
- token_adapter: int32 [49152], P('dp'), may hold values from -1 to 191, as said below
- owner_map: int32 [192], replicated, may hold values from 0 to 191, each once
Outputs:
- gradient_wrt_input: bfloat16 [49152, 5120], P('dp', 'tensor')
- grad_b: float32 [192, 16, 1024], P('dp', None, 'tensor')
The draws below stay inside these ranges and needn't reach their ends.
Inputs may be any that keep to these rules, and one draw needn't show every extreme that they name: `block_adapter`: each block of 128 rows serves one adapter; some adapters serve many blocks. `token_adapter`: in each block the first rows (at least 32 of them) carry the block's adapter and the rest are padding with -1. A permutation; adapter e stands at slot owner_map[e], on dp index owner_map[e] // 2.
All inputs are finite; a program needn't handle non-finite values.
Results may differ from the reference program's by a relative error of at most 0.0045.
Values may be sent and summed in bfloat16 or wider, within the bound.
No kernel may reach another device: no remote copies, remote signals or barrier semaphores. Data moves between devices by JAX's collectives and lax.ppermute only.
A program may use at most 32 MiB of HBM per device.

```python
import jax
import jax.numpy as jnp
from jax import lax

D = 5120
RANK = 16
BLK = 128
KOUT = 1024
ADAPTERS = 192
BLOCKS = 384
TOKENS = 49152


def block_choice(key):
    first, second, third, mixer = jax.random.split(key, 4)
    picked = jax.random.randint(first, (BLOCKS,), 0, ADAPTERS)
    picked = jnp.minimum(picked, jax.random.randint(second, (BLOCKS,), 0, ADAPTERS))
    picked = jnp.minimum(picked, jax.random.randint(third, (BLOCKS,), 0, ADAPTERS))
    relabel = jax.random.permutation(mixer, ADAPTERS)
    return relabel[picked].astype(jnp.int32)


def draw_block_adapter(key, part):
    block_ids = block_choice(key)
    return block_ids


def draw_token_adapter(key, part):
    block_ids = block_choice(key)
    key = jax.random.fold_in(key, 7)
    live_counts = jax.random.randint(key, (BLOCKS,), BLK // 4, BLK + 1)
    position = jnp.arange(BLK, dtype=jnp.int32)[None, :]
    labels = jnp.where(position < live_counts[:, None], block_ids[:, None], -1)
    return labels.reshape(BLOCKS * BLK).astype(jnp.int32)


def block_levels(stream_key, extent, shards, smallest, largest):
    def one(axis_at, shards_of):
        steps = jax.random.uniform(jax.random.fold_in(jax.random.fold_in(stream_key, 6), axis_at), (shards_of,), jnp.float32, smallest / len(shards), largest / len(shards))
        return jnp.repeat(jnp.exp(steps), extent[axis_at] // shards_of).reshape((-1,) + (1,) * (len(extent) - axis_at - 1))

    gain = one(*shards[0])
    for cut in shards[1:]:
        gain = gain * one(*cut)
    return gain


def centred(stream_key, shape, width, bound, shards=(), kind=jnp.bfloat16):
    values = width * jax.random.normal(stream_key, shape, jnp.float32)
    if shards:
        values = values * block_levels(stream_key, shape, shards, -0.22, 0.18)
    return jnp.clip(values, -bound, bound).astype(kind)


def setup_inputs(seed: int = 0) -> dict:
    keys = jax.random.split(jax.random.key(seed), 9)
    return {
        "inputs": centred(keys[0], (TOKENS, D), 1.0, 6.0, ((0, 96), (1, 8))),
        "cotangent": centred(keys[1], (TOKENS, KOUT), 0.25, 1.5, ((0, 96), (1, 8))),
        "base_weight": centred(keys[2], (D, KOUT), D ** -0.5, 0.078125, ((0, 8),)),
        "down_a": centred(keys[3], (ADAPTERS, D, RANK), D ** -0.5, 0.078125, ((0, 96), (1, 8))),
        "up_b": centred(keys[4], (ADAPTERS, RANK, KOUT), RANK ** -0.5, 1.5, ((0, 96), (2, 8))),
        "block_adapter": draw_block_adapter(jax.random.fold_in(keys[8], 71), 0),
        "token_adapter": draw_token_adapter(jax.random.fold_in(keys[8], 71), 0),
        "owner_map": jax.random.permutation(keys[7], ADAPTERS).astype(jnp.int32),
    }


adapter_scale_factor = 2.0


def reference(inputs, cotangent, base_weight, down_a, up_b, block_adapter, token_adapter, owner_map):
    slot_ids = owner_map[block_adapter].astype(jnp.int32)
    live_rows = (token_adapter >= 0).astype(jnp.float32).reshape(BLOCKS, BLK, 1)
    input_row_blocks = inputs.reshape(BLOCKS, BLK, D)
    g_blocks = cotangent.reshape(BLOCKS, BLK, KOUT)
    contract_last = (((1,), (1,)), ((), ()))

    def one_block(operands):
        x_block, g_block, mask_block, slot = operands
        selected_down_matrix = lax.dynamic_index_in_dim(down_a, slot, 0, keepdims=False)
        up_sel = lax.dynamic_index_in_dim(up_b, slot, 0, keepdims=False)
        low_rank_product = (jnp.dot(x_block, selected_down_matrix, preferred_element_type=jnp.float32) * mask_block).astype(jnp.bfloat16)
        masked_rows = (g_block.astype(jnp.float32) * mask_block).astype(jnp.bfloat16)
        hidden_features = lax.dot_general(masked_rows, up_sel, contract_last, preferred_element_type=jnp.float32).astype(jnp.bfloat16)
        frozen_path_gradient = lax.dot_general(masked_rows, base_weight, contract_last, preferred_element_type=jnp.float32)
        adapter_path_gradient = lax.dot_general(hidden_features, selected_down_matrix, contract_last, preferred_element_type=jnp.float32)
        block_input_gradient = (frozen_path_gradient + adapter_scale_factor * adapter_path_gradient).astype(jnp.bfloat16)
        block_partial_term = adapter_scale_factor * jnp.dot(low_rank_product.T, masked_rows, preferred_element_type=jnp.float32)
        return block_input_gradient, block_partial_term

    grads, block_partial_terms = lax.map(one_block, (input_row_blocks, g_blocks, live_rows, slot_ids))
    grad_b = jnp.zeros((ADAPTERS, RANK, KOUT), jnp.float32).at[slot_ids].add(block_partial_terms)
    return grads.reshape(TOKENS, D), grad_b
```

```python
import jax
import jax.numpy as jnp
from jax import lax
from jax.sharding import PartitionSpec as P

adapter_scale_factor = 2.0
LINE = 8
LANES = 128


def on_device(
    inputs, cotangent, base_weight, down_a, up_b, block_adapter, token_adapter, owner_map
):
    row_count, dpiece = inputs.shape
    kpiece = cotangent.shape[1]
    block_count = block_adapter.shape[0]
    blk_rows = row_count // block_count
    nadapt = owner_map.shape[0]
    own_slots, _, rank = down_a.shape
    dp = lax.axis_size("dp")
    tensor = lax.axis_size("tensor")
    columns = dp // LINE
    chunks = dpiece // LANES
    y_groups = [[z * LINE + y for y in range(LINE)] for z in range(columns)]
    z_groups = [[z * LINE + y for z in range(columns)] for y in range(LINE)]
    my_y = lax.axis_index("dp") % LINE
    my_row = lax.axis_index("dp") // LINE

    full_cotangent = lax.all_gather(cotangent, "tensor", axis=1, tiled=True)

    matches = block_adapter[:, None] == jnp.arange(nadapt, dtype=jnp.int32)[None, :]
    slot_ids = jnp.sum(jnp.where(matches, owner_map[None, :], 0), axis=1)
    live = (token_adapter >= 0).astype(jnp.float32)

    weights = jnp.concatenate([down_a.transpose(0, 2, 1), up_b], axis=2)
    pieces = weights.reshape(own_slots, rank, chunks + 1, LANES).transpose(2, 1, 0, 3)
    pieces = pieces.reshape(dp, own_slots, LANES)
    id_row = jnp.pad(slot_ids, (0, LANES - block_count)).astype(jnp.bfloat16)
    id_rows = jnp.broadcast_to(id_row, (dp, own_slots, LANES))
    table = lax.all_to_all(jnp.concatenate([pieces, id_rows], axis=1), "dp", 0, 0)
    all_slots = table[:, own_slots, :block_count].astype(jnp.int32)
    table = table[:, :own_slots].reshape(dp * own_slots, LANES)

    onehot = (
        all_slots.reshape(-1, 1) == jnp.arange(dp * own_slots, dtype=jnp.int32)[None, :]
    ).astype(jnp.bfloat16)
    picked = jnp.dot(onehot, table, preferred_element_type=jnp.float32).astype(jnp.bfloat16)
    picked = lax.all_to_all(picked.reshape(dp, block_count, LANES), "dp", 0, 0)
    picked = picked.reshape(chunks + 1, rank, block_count, LANES)
    down_sel = picked[:chunks].transpose(2, 1, 0, 3).reshape(block_count, rank, dpiece)
    up_sel = picked[chunks].transpose(1, 0, 2)

    input_blocks = inputs.reshape(block_count, blk_rows, dpiece)
    g_blocks = cotangent.reshape(block_count, blk_rows, kpiece)
    low_part = jnp.einsum("brd,bnd->brn", down_sel, input_blocks, preferred_element_type=jnp.float32)
    hid_part = jnp.einsum("brk,bnk->brn", up_sel, g_blocks, preferred_element_type=jnp.float32)
    part = jnp.concatenate([low_part, hid_part], axis=1).astype(jnp.bfloat16)
    part = lax.all_to_all(jnp.broadcast_to(part, (tensor,) + part.shape), "tensor", 0, 0)
    total = jnp.sum(part.astype(jnp.float32), axis=0) * live.reshape(block_count, 1, blk_rows)
    total = total.astype(jnp.bfloat16)
    low_rank, hidden = total[:, :rank], total[:, rank:]

    terms = adapter_scale_factor * jnp.einsum(
        "brn,bno->bro", low_rank, g_blocks, preferred_element_type=jnp.float32
    )
    terms = terms.astype(jnp.bfloat16)
    terms = lax.all_to_all(
        jnp.broadcast_to(terms, (LINE,) + terms.shape), "dp", 0, 0, axis_index_groups=y_groups
    )
    terms = terms.reshape(LINE * block_count, rank, kpiece)
    row_slots = lax.dynamic_slice_in_dim(all_slots, my_row * LINE, LINE, 0).reshape(-1)
    column_slots = (
        jnp.arange(columns, dtype=jnp.int32)[:, None] * (LINE * own_slots)
        + my_y * own_slots
        + jnp.arange(own_slots, dtype=jnp.int32)[None, :]
    ).reshape(-1)
    owner_match = (column_slots[:, None] == row_slots[None, :]).astype(jnp.bfloat16)
    sums = jnp.einsum("sb,bro->sro", owner_match, terms, preferred_element_type=jnp.float32)
    sums = lax.all_to_all(
        sums.reshape(columns, own_slots, rank, kpiece), "dp", 0, 0, axis_index_groups=z_groups
    )
    grad_b = jnp.sum(sums, axis=0)

    frozen = lax.dot_general(
        full_cotangent, base_weight, (((1,), (1,)), ((), ())), preferred_element_type=jnp.float32
    )
    adapter = jnp.einsum(
        "brn,brd->bnd", hidden, down_sel, preferred_element_type=jnp.float32
    ).reshape(row_count, dpiece)
    gradient = (frozen * live[:, None] + adapter_scale_factor * adapter).astype(jnp.bfloat16)
    return (gradient, grad_b)


def solution(mesh):
    in_specs = (
        P("dp", "tensor"),
        P("dp", "tensor"),
        P("tensor", None),
        P("dp", "tensor", None),
        P("dp", None, "tensor"),
        P("dp"),
        P("dp"),
        P(),
    )
    out_specs = (P("dp", "tensor"), P("dp", None, "tensor"))
    return jax.shard_map(
        on_device, mesh=mesh, in_specs=in_specs, out_specs=out_specs, check_vma=False
    )
```

```python
import jax
import jax.numpy as jnp
from jax import lax
from jax.sharding import PartitionSpec as P

adapter_scale_factor = 2.0
LINE = 8
LANES = 128
CORES = 2


def on_device(
    inputs, cotangent, base_weight, down_a, up_b, block_adapter, token_adapter, owner_map
):
    row_count, dpiece = inputs.shape
    kpiece = cotangent.shape[1]
    block_count = block_adapter.shape[0]
    blk_rows = row_count // block_count
    nadapt = owner_map.shape[0]
    own_slots, _, rank = down_a.shape
    dp = lax.axis_size("dp")
    tensor = lax.axis_size("tensor")
    columns = dp // LINE
    chunks = dpiece // LANES
    y_groups = [[z * LINE + y for y in range(LINE)] for z in range(columns)]
    z_groups = [[z * LINE + y for z in range(columns)] for y in range(LINE)]
    my_y = lax.axis_index("dp") % LINE
    my_row = lax.axis_index("dp") // LINE

    my_tensor = lax.axis_index("tensor")
    my_x, my_core = my_tensor // CORES, my_tensor % CORES
    last = tensor - 1

    def both(mine, other, mine_first):
        return jnp.where(mine_first, jnp.concatenate([mine, other], axis=1), jnp.concatenate([other, mine], axis=1))

    near = [(i, i ^ 1) for i in range(tensor)]
    pair = [(i, i ^ CORES) for i in range(tensor)]
    far = [(i, (last - i) ^ 1) for i in range(tensor)]
    held = both(cotangent, lax.ppermute(cotangent, "tensor", near), my_core == 0)
    held = both(held, lax.ppermute(held, "tensor", pair), my_x % 2 == 0)
    full_cotangent = both(held, lax.ppermute(held, "tensor", far), my_x < 2)

    matches = block_adapter[:, None] == jnp.arange(nadapt, dtype=jnp.int32)[None, :]
    slot_ids = jnp.sum(jnp.where(matches, owner_map[None, :], 0), axis=1)
    live = (token_adapter >= 0).astype(jnp.float32)

    weights = jnp.concatenate([down_a.transpose(0, 2, 1), up_b], axis=2)
    pieces = weights.reshape(own_slots, rank, chunks + 1, LANES).transpose(2, 1, 0, 3)
    pieces = pieces.reshape(dp, own_slots, LANES)
    id_row = jnp.pad(slot_ids, (0, LANES - block_count)).astype(jnp.bfloat16)
    id_rows = jnp.broadcast_to(id_row, (dp, own_slots, LANES))
    table = lax.all_to_all(jnp.concatenate([pieces, id_rows], axis=1), "dp", 0, 0)
    all_slots = table[:, own_slots, :block_count].astype(jnp.int32)
    table = table[:, :own_slots].reshape(dp * own_slots, LANES)

    onehot = (
        all_slots.reshape(-1, 1) == jnp.arange(dp * own_slots, dtype=jnp.int32)[None, :]
    ).astype(jnp.bfloat16)
    picked = jnp.dot(onehot, table, preferred_element_type=jnp.float32).astype(jnp.bfloat16)
    picked = lax.all_to_all(picked.reshape(dp, block_count, LANES), "dp", 0, 0)
    picked = picked.reshape(chunks + 1, rank, block_count, LANES)
    down_sel = picked[:chunks].transpose(2, 1, 0, 3).reshape(block_count, rank, dpiece)
    up_sel = picked[chunks].transpose(1, 0, 2)

    input_blocks = inputs.reshape(block_count, blk_rows, dpiece)
    g_blocks = cotangent.reshape(block_count, blk_rows, kpiece)
    low_part = jnp.einsum("brd,bnd->brn", down_sel, input_blocks, preferred_element_type=jnp.float32)
    hid_part = jnp.einsum("brk,bnk->brn", up_sel, g_blocks, preferred_element_type=jnp.float32)
    part = jnp.concatenate([low_part, hid_part], axis=1).astype(jnp.bfloat16)
    part = lax.all_to_all(jnp.broadcast_to(part, (tensor,) + part.shape), "tensor", 0, 0)
    total = jnp.sum(part.astype(jnp.float32), axis=0) * live.reshape(block_count, 1, blk_rows)
    total = total.astype(jnp.bfloat16)
    low_rank, hidden = total[:, :rank], total[:, rank:]

    terms = adapter_scale_factor * jnp.einsum(
        "brn,bno->bro", low_rank, g_blocks, preferred_element_type=jnp.float32
    )
    terms = terms.astype(jnp.bfloat16)
    terms = lax.all_to_all(
        jnp.broadcast_to(terms, (LINE,) + terms.shape), "dp", 0, 0, axis_index_groups=y_groups
    )
    terms = terms.reshape(LINE * block_count, rank, kpiece)
    row_slots = lax.dynamic_slice_in_dim(all_slots, my_row * LINE, LINE, 0).reshape(-1)
    column_slots = (
        jnp.arange(columns, dtype=jnp.int32)[:, None] * (LINE * own_slots)
        + my_y * own_slots
        + jnp.arange(own_slots, dtype=jnp.int32)[None, :]
    ).reshape(-1)
    owner_match = (column_slots[:, None] == row_slots[None, :]).astype(jnp.bfloat16)
    sums = jnp.einsum("sb,bro->sro", owner_match, terms, preferred_element_type=jnp.float32)
    sums = lax.all_to_all(
        sums.reshape(columns, own_slots, rank, kpiece), "dp", 0, 0, axis_index_groups=z_groups
    )
    grad_b = jnp.sum(sums, axis=0)

    frozen = lax.dot_general(
        full_cotangent, base_weight, (((1,), (1,)), ((), ())), preferred_element_type=jnp.float32
    )
    adapter = jnp.einsum(
        "brn,brd->bnd", hidden, down_sel, preferred_element_type=jnp.float32
    ).reshape(row_count, dpiece)
    gradient = (frozen * live[:, None] + adapter_scale_factor * adapter).astype(jnp.bfloat16)
    return (gradient, grad_b)


def solution(mesh):
    in_specs = (
        P("dp", "tensor"),
        P("dp", "tensor"),
        P("tensor", None),
        P("dp", "tensor", None),
        P("dp", None, "tensor"),
        P("dp"),
        P("dp"),
        P(),
    )
    out_specs = (P("dp", "tensor"), P("dp", None, "tensor"))
    return jax.shard_map(
        on_device, mesh=mesh, in_specs=in_specs, out_specs=out_specs, check_vma=False
    )
```

```python
import jax
import jax.numpy as jnp
from jax import lax
from jax.experimental import pallas as pl
from jax.experimental.pallas import tpu as pltpu
from jax.sharding import PartitionSpec as P

adapter_scale_factor = 2.0
LINE = 8
LANES = 128
CORES = 2


SPARE = 4


def pack_kernel(adapter_ref, owner_ref, down_ref, up_ref, out_ref):
    slots, rank, dpiece = down_ref.shape
    blocks = adapter_ref.shape[0]
    rows = rank * SPARE
    at = lax.broadcasted_iota(jnp.int32, (rows, slots * rank), 0)
    source = lax.broadcasted_iota(jnp.int32, (rows, slots * rank), 1)
    spread = (source == (at % SPARE) * rank + at // SPARE).astype(jnp.bfloat16)
    kind = lax.broadcasted_iota(jnp.int32, (rows, LANES), 0) % SPARE
    lane = lax.broadcasted_iota(jnp.int32, (rows, LANES), 1)
    numbers = jnp.zeros((rows, LANES), jnp.float32)
    for b in range(blocks):
        slot = owner_ref[adapter_ref[b]].astype(jnp.float32)
        numbers = jnp.where((kind == slots) & (lane == b), slot, numbers)
    down = jnp.concatenate([down_ref[j] for j in range(slots)], axis=0)
    up = jnp.concatenate([up_ref[j] for j in range(slots)], axis=0)
    for c in range(dpiece // LANES + 1):
        chunk = up if c == dpiece // LANES else down[:, c * LANES : (c + 1) * LANES]
        mixed = jnp.dot(spread, chunk, preferred_element_type=jnp.float32)
        out_ref[c * rows : (c + 1) * rows, :] = (mixed + numbers).astype(jnp.bfloat16)


def pack(block_adapter, owner_map, down_rows, up_b):
    _, rank, dpiece = down_rows.shape
    smem = pl.BlockSpec(memory_space=pltpu.SMEM)
    vmem = pl.BlockSpec(memory_space=pltpu.VMEM)
    return pl.pallas_call(
        pack_kernel,
        out_shape=jax.ShapeDtypeStruct((SPARE * rank * (dpiece // LANES + 1), LANES), jnp.bfloat16),
        in_specs=[smem, smem, vmem, vmem],
        out_specs=vmem,
    )(block_adapter, owner_map, down_rows, up_b)


def on_device(
    inputs, cotangent, base_weight, down_a, up_b, block_adapter, token_adapter, owner_map
):
    row_count, dpiece = inputs.shape
    kpiece = cotangent.shape[1]
    block_count = block_adapter.shape[0]
    blk_rows = row_count // block_count
    own_slots, _, rank = down_a.shape
    dp = lax.axis_size("dp")
    tensor = lax.axis_size("tensor")
    columns = dp // LINE
    chunks = dpiece // LANES
    y_groups = [[z * LINE + y for y in range(LINE)] for z in range(columns)]
    z_groups = [[z * LINE + y for z in range(columns)] for y in range(LINE)]
    my_y = lax.axis_index("dp") % LINE
    my_row = lax.axis_index("dp") // LINE

    my_tensor = lax.axis_index("tensor")
    my_x, my_core = my_tensor // CORES, my_tensor % CORES
    last = tensor - 1

    def both(mine, other, mine_first):
        return jnp.where(mine_first, jnp.concatenate([mine, other], axis=1), jnp.concatenate([other, mine], axis=1))

    near = [(i, i ^ 1) for i in range(tensor)]
    pair = [(i, i ^ CORES) for i in range(tensor)]
    far = [(i, (last - i) ^ 1) for i in range(tensor)]
    held = both(cotangent, lax.ppermute(cotangent, "tensor", near), my_core == 0)
    held = both(held, lax.ppermute(held, "tensor", pair), my_x % 2 == 0)
    full_cotangent = both(held, lax.ppermute(held, "tensor", far), my_x < 2)

    live = (token_adapter >= 0).astype(jnp.float32)

    pieces = pack(block_adapter, owner_map, down_a.transpose(0, 2, 1), up_b)
    table = lax.all_to_all(pieces.reshape(dp, SPARE, LANES), "dp", 0, 0)
    all_slots = table[:, own_slots, :block_count].astype(jnp.int32)
    table = table[:, :own_slots].reshape(dp * own_slots, LANES)

    onehot = (
        all_slots.reshape(-1, 1) == jnp.arange(dp * own_slots, dtype=jnp.int32)[None, :]
    ).astype(jnp.bfloat16)
    picked = jnp.dot(onehot, table, preferred_element_type=jnp.float32).astype(jnp.bfloat16)
    picked = lax.all_to_all(picked.reshape(dp, block_count, LANES), "dp", 0, 0)
    picked = picked.reshape(chunks + 1, rank, block_count, LANES)
    down_sel = picked[:chunks].transpose(2, 1, 0, 3).reshape(block_count, rank, dpiece)
    up_sel = picked[chunks].transpose(1, 0, 2)

    input_blocks = inputs.reshape(block_count, blk_rows, dpiece)
    g_blocks = cotangent.reshape(block_count, blk_rows, kpiece)
    low_part = jnp.einsum("brd,bnd->brn", down_sel, input_blocks, preferred_element_type=jnp.float32)
    hid_part = jnp.einsum("brk,bnk->brn", up_sel, g_blocks, preferred_element_type=jnp.float32)
    part = jnp.concatenate([low_part, hid_part], axis=1).astype(jnp.bfloat16)
    part = lax.all_to_all(jnp.broadcast_to(part, (tensor,) + part.shape), "tensor", 0, 0)
    total = jnp.sum(part.astype(jnp.float32), axis=0) * live.reshape(block_count, 1, blk_rows)
    total = total.astype(jnp.bfloat16)
    low_rank, hidden = total[:, :rank], total[:, rank:]

    terms = adapter_scale_factor * jnp.einsum(
        "brn,bno->bro", low_rank, g_blocks, preferred_element_type=jnp.float32
    )
    terms = terms.astype(jnp.bfloat16)
    terms = lax.all_to_all(
        jnp.broadcast_to(terms, (LINE,) + terms.shape), "dp", 0, 0, axis_index_groups=y_groups
    )
    terms = terms.reshape(LINE * block_count, rank, kpiece)
    row_slots = lax.dynamic_slice_in_dim(all_slots, my_row * LINE, LINE, 0).reshape(-1)
    column_slots = (
        jnp.arange(columns, dtype=jnp.int32)[:, None] * (LINE * own_slots)
        + my_y * own_slots
        + jnp.arange(own_slots, dtype=jnp.int32)[None, :]
    ).reshape(-1)
    owner_match = (column_slots[:, None] == row_slots[None, :]).astype(jnp.bfloat16)
    sums = jnp.einsum("sb,bro->sro", owner_match, terms, preferred_element_type=jnp.float32)
    sums = lax.all_to_all(
        sums.astype(jnp.bfloat16).reshape(columns, own_slots, rank, kpiece), "dp", 0, 0, axis_index_groups=z_groups
    )
    grad_b = jnp.sum(sums.astype(jnp.float32), axis=0)

    frozen = lax.dot_general(
        full_cotangent, base_weight, (((1,), (1,)), ((), ())), preferred_element_type=jnp.float32
    )
    adapter = jnp.einsum(
        "brn,brd->bnd", hidden, down_sel, preferred_element_type=jnp.float32
    ).reshape(row_count, dpiece)
    gradient = (frozen * live[:, None] + adapter_scale_factor * adapter).astype(jnp.bfloat16)
    return (gradient, grad_b)


def solution(mesh):
    in_specs = (
        P("dp", "tensor"),
        P("dp", "tensor"),
        P("tensor", None),
        P("dp", "tensor", None),
        P("dp", None, "tensor"),
        P("dp"),
        P("dp"),
        P(),
    )
    out_specs = (P("dp", "tensor"), P("dp", None, "tensor"))
    return jax.shard_map(
        on_device, mesh=mesh, in_specs=in_specs, out_specs=out_specs, check_vma=False
    )
```

```python
import functools

import jax
import jax.numpy as jnp
from jax import lax
from jax.experimental import pallas as pl
from jax.experimental.pallas import tpu as pltpu
from jax.sharding import PartitionSpec as P

adapter_scale_factor = 2.0
LINE = 8
FIRST_Z = 9
FIRST_Y = 4
LANES = 128
CORES = 2


SPARE = 4


def listed(z, y, columns):
    return lax.rem(z + (columns - FIRST_Z), columns), lax.rem(y + (LINE - FIRST_Y), LINE)


def listed_slot(slot, slots, columns):
    owner = lax.div(slot, slots)
    z, y = listed(lax.div(owner, LINE), lax.rem(owner, LINE), columns)
    return (z * LINE + y) * slots + lax.rem(slot, slots)


def pack_kernel(columns, adapter_ref, owner_ref, down_ref, up_ref, out_ref):
    slots, rank, dpiece = down_ref.shape
    blocks = adapter_ref.shape[0]
    rows = rank * SPARE
    at = lax.broadcasted_iota(jnp.int32, (rows, slots * rank), 0)
    source = lax.broadcasted_iota(jnp.int32, (rows, slots * rank), 1)
    spread = (source == (at % SPARE) * rank + at // SPARE).astype(jnp.bfloat16)
    kind = lax.broadcasted_iota(jnp.int32, (rows, LANES), 0) % SPARE
    lane = lax.broadcasted_iota(jnp.int32, (rows, LANES), 1)
    numbers = jnp.zeros((rows, LANES), jnp.float32)
    for b in range(blocks):
        slot = listed_slot(owner_ref[adapter_ref[b]], slots, columns).astype(jnp.float32)
        numbers = jnp.where((kind == slots) & (lane == b), slot, numbers)
    down = jnp.concatenate([down_ref[j] for j in range(slots)], axis=0)
    up = jnp.concatenate([up_ref[j] for j in range(slots)], axis=0)
    for c in range(dpiece // LANES + 1):
        chunk = up if c == dpiece // LANES else down[:, c * LANES : (c + 1) * LANES]
        mixed = jnp.dot(spread, chunk, preferred_element_type=jnp.float32)
        out_ref[c * rows : (c + 1) * rows, :] = (mixed + numbers).astype(jnp.bfloat16)


def pack(columns, block_adapter, owner_map, down_rows, up_b):
    _, rank, dpiece = down_rows.shape
    smem = pl.BlockSpec(memory_space=pltpu.SMEM)
    vmem = pl.BlockSpec(memory_space=pltpu.VMEM)
    return pl.pallas_call(
        functools.partial(pack_kernel, columns),
        out_shape=jax.ShapeDtypeStruct((SPARE * rank * (dpiece // LANES + 1), LANES), jnp.bfloat16),
        in_specs=[smem, smem, vmem, vmem],
        out_specs=vmem,
    )(block_adapter, owner_map, down_rows, up_b)


def on_device(
    inputs, cotangent, base_weight, down_a, up_b, block_adapter, token_adapter, owner_map
):
    row_count, dpiece = inputs.shape
    kpiece = cotangent.shape[1]
    block_count = block_adapter.shape[0]
    blk_rows = row_count // block_count
    own_slots, _, rank = down_a.shape
    dp = lax.axis_size("dp")
    tensor = lax.axis_size("tensor")
    columns = dp // LINE
    chunks = dpiece // LANES
    z_list = [(FIRST_Z + z) % columns for z in range(columns)]
    y_list = [(FIRST_Y + y) % LINE for y in range(LINE)]
    plane = [[z * LINE + y for z in z_list for y in y_list]]
    y_groups = [[z * LINE + y for y in y_list] for z in range(columns)]
    z_groups = [[z * LINE + y for z in z_list] for y in range(LINE)]
    my_dp = lax.axis_index("dp")
    my_row, my_y = listed(lax.div(my_dp, LINE), lax.rem(my_dp, LINE), columns)

    my_tensor = lax.axis_index("tensor")
    my_x, my_core = my_tensor // CORES, my_tensor % CORES
    last = tensor - 1

    def both(mine, other, mine_first):
        return jnp.where(mine_first, jnp.concatenate([mine, other], axis=1), jnp.concatenate([other, mine], axis=1))

    near = [(i, i ^ 1) for i in range(tensor)]
    pair = [(i, i ^ CORES) for i in range(tensor)]
    far = [(i, (last - i) ^ 1) for i in range(tensor)]
    held = both(cotangent, lax.ppermute(cotangent, "tensor", near), my_core == 0)
    held = both(held, lax.ppermute(held, "tensor", pair), my_x % 2 == 0)
    full_cotangent = both(held, lax.ppermute(held, "tensor", far), my_x < 2)

    live = (token_adapter >= 0).astype(jnp.float32)

    pieces = pack(columns, block_adapter, owner_map, down_a.transpose(0, 2, 1), up_b)
    table = lax.all_to_all(
        pieces.reshape(dp, SPARE, LANES), "dp", 0, 0, axis_index_groups=plane
    )
    all_slots = table[:, own_slots, :block_count].astype(jnp.int32)
    table = table[:, :own_slots].reshape(dp * own_slots, LANES)

    onehot = (
        all_slots.reshape(-1, 1) == jnp.arange(dp * own_slots, dtype=jnp.int32)[None, :]
    ).astype(jnp.bfloat16)
    picked = jnp.dot(onehot, table, preferred_element_type=jnp.float32).astype(jnp.bfloat16)
    picked = lax.all_to_all(
        picked.reshape(dp, block_count, LANES), "dp", 0, 0, axis_index_groups=plane
    )
    picked = picked.reshape(chunks + 1, rank, block_count, LANES)
    down_sel = picked[:chunks].transpose(2, 1, 0, 3).reshape(block_count, rank, dpiece)
    up_sel = picked[chunks].transpose(1, 0, 2)

    input_blocks = inputs.reshape(block_count, blk_rows, dpiece)
    g_blocks = cotangent.reshape(block_count, blk_rows, kpiece)
    low_part = jnp.einsum("brd,bnd->brn", down_sel, input_blocks, preferred_element_type=jnp.float32)
    hid_part = jnp.einsum("brk,bnk->brn", up_sel, g_blocks, preferred_element_type=jnp.float32)
    part = jnp.concatenate([low_part, hid_part], axis=1).astype(jnp.bfloat16)
    part = lax.all_to_all(jnp.broadcast_to(part, (tensor,) + part.shape), "tensor", 0, 0)
    total = jnp.sum(part.astype(jnp.float32), axis=0) * live.reshape(block_count, 1, blk_rows)
    total = total.astype(jnp.bfloat16)
    low_rank, hidden = total[:, :rank], total[:, rank:]

    terms = adapter_scale_factor * jnp.einsum(
        "brn,bno->bro", low_rank, g_blocks, preferred_element_type=jnp.float32
    )
    terms = terms.astype(jnp.bfloat16)
    terms = lax.all_to_all(
        jnp.broadcast_to(terms, (LINE,) + terms.shape), "dp", 0, 0, axis_index_groups=y_groups
    )
    terms = terms.reshape(LINE * block_count, rank, kpiece)
    row_slots = lax.dynamic_slice_in_dim(all_slots, my_row * LINE, LINE, 0).reshape(-1)
    column_slots = (
        jnp.arange(columns, dtype=jnp.int32)[:, None] * (LINE * own_slots)
        + my_y * own_slots
        + jnp.arange(own_slots, dtype=jnp.int32)[None, :]
    ).reshape(-1)
    owner_match = (column_slots[:, None] == row_slots[None, :]).astype(jnp.bfloat16)
    sums = jnp.einsum("sb,bro->sro", owner_match, terms, preferred_element_type=jnp.float32)
    sums = lax.all_to_all(
        sums.astype(jnp.bfloat16).reshape(columns, own_slots, rank, kpiece), "dp", 0, 0, axis_index_groups=z_groups
    )
    grad_b = jnp.sum(sums.astype(jnp.float32), axis=0)

    frozen = lax.dot_general(
        full_cotangent, base_weight, (((1,), (1,)), ((), ())), preferred_element_type=jnp.float32
    )
    adapter = jnp.einsum(
        "brn,brd->bnd", hidden, down_sel, preferred_element_type=jnp.float32
    ).reshape(row_count, dpiece)
    gradient = (frozen * live[:, None] + adapter_scale_factor * adapter).astype(jnp.bfloat16)
    return (gradient, grad_b)


def solution(mesh):
    in_specs = (
        P("dp", "tensor"),
        P("dp", "tensor"),
        P("tensor", None),
        P("dp", "tensor", None),
        P("dp", None, "tensor"),
        P("dp"),
        P("dp"),
        P(),
    )
    out_specs = (P("dp", "tensor"), P("dp", None, "tensor"))
    return jax.shard_map(
        on_device, mesh=mesh, in_specs=in_specs, out_specs=out_specs, check_vma=False
    )
```

```python
import functools

import jax
import jax.numpy as jnp
from jax import lax
from jax.experimental import pallas as pl
from jax.experimental.pallas import tpu as pltpu
from jax.sharding import PartitionSpec as P

adapter_scale_factor = 2.0
LINE = 8
FIRST_Z = 9
FIRST_Y = 4
LAST_Z = 7
FIRST_X = 2
LANES = 128
CORES = 2


SPARE = 4


def far_first(at, first, extent):
    past = lax.rem(at + (extent - first), extent) - extent // 2
    return lax.select(past >= 0, 2 * past + 1, lax.rem(-2 * past, extent))


def far_first_list(first, extent):
    aside = [first]
    for step in range(extent - 1):
        past = (step + 1) // 2
        past = past if step % 2 == 0 else -past
        aside.append((first + extent // 2 + past) % extent)
    return aside


def listed(z, y, columns):
    return far_first(z, FIRST_Z, columns), far_first(y, FIRST_Y, LINE)


def listed_slot(slot, slots, columns):
    owner = lax.div(slot, slots)
    z, y = listed(lax.div(owner, LINE), lax.rem(owner, LINE), columns)
    return (z * LINE + y) * slots + lax.rem(slot, slots)


def pack_kernel(columns, adapter_ref, owner_ref, down_ref, up_ref, out_ref):
    slots, rank, dpiece = down_ref.shape
    blocks = adapter_ref.shape[0]
    rows = rank * SPARE
    at = lax.broadcasted_iota(jnp.int32, (rows, slots * rank), 0)
    source = lax.broadcasted_iota(jnp.int32, (rows, slots * rank), 1)
    spread = (source == (at % SPARE) * rank + at // SPARE).astype(jnp.bfloat16)
    kind = lax.broadcasted_iota(jnp.int32, (rows, LANES), 0) % SPARE
    lane = lax.broadcasted_iota(jnp.int32, (rows, LANES), 1)
    numbers = jnp.zeros((rows, LANES), jnp.float32)
    for b in range(blocks):
        slot = listed_slot(owner_ref[adapter_ref[b]], slots, columns).astype(jnp.float32)
        numbers = jnp.where((kind == slots) & (lane == b), slot, numbers)
    down = jnp.concatenate([down_ref[j] for j in range(slots)], axis=0)
    up = jnp.concatenate([up_ref[j] for j in range(slots)], axis=0)
    for c in range(dpiece // LANES + 1):
        chunk = up if c == dpiece // LANES else down[:, c * LANES : (c + 1) * LANES]
        mixed = jnp.dot(spread, chunk, preferred_element_type=jnp.float32)
        out_ref[c * rows : (c + 1) * rows, :] = (mixed + numbers).astype(jnp.bfloat16)


def pack(columns, block_adapter, owner_map, down_rows, up_b):
    _, rank, dpiece = down_rows.shape
    smem = pl.BlockSpec(memory_space=pltpu.SMEM)
    vmem = pl.BlockSpec(memory_space=pltpu.VMEM)
    return pl.pallas_call(
        functools.partial(pack_kernel, columns),
        out_shape=jax.ShapeDtypeStruct((SPARE * rank * (dpiece // LANES + 1), LANES), jnp.bfloat16),
        in_specs=[smem, smem, vmem, vmem],
        out_specs=vmem,
    )(block_adapter, owner_map, down_rows, up_b)


def on_device(
    inputs, cotangent, base_weight, down_a, up_b, block_adapter, token_adapter, owner_map
):
    row_count, dpiece = inputs.shape
    kpiece = cotangent.shape[1]
    block_count = block_adapter.shape[0]
    blk_rows = row_count // block_count
    own_slots, _, rank = down_a.shape
    dp = lax.axis_size("dp")
    tensor = lax.axis_size("tensor")
    columns = dp // LINE
    chunks = dpiece // LANES
    z_list = far_first_list(FIRST_Z, columns)
    y_list = far_first_list(FIRST_Y, LINE)
    plane = [[z * LINE + y for z in z_list for y in y_list]]
    y_groups = [[z * LINE + y for y in y_list] for z in range(columns)]
    last_list = far_first_list(LAST_Z, columns)
    z_groups = [[z * LINE + y for z in last_list] for y in range(LINE)]
    x_list = far_first_list(FIRST_X, tensor // CORES)
    t_group = [[x * CORES + core for x in x_list for core in reversed(range(CORES))]]
    my_dp = lax.axis_index("dp")
    my_row, my_y = listed(lax.div(my_dp, LINE), lax.rem(my_dp, LINE), columns)

    my_tensor = lax.axis_index("tensor")
    my_x, my_core = my_tensor // CORES, my_tensor % CORES
    last = tensor - 1

    def both(mine, other, mine_first):
        return jnp.where(mine_first, jnp.concatenate([mine, other], axis=1), jnp.concatenate([other, mine], axis=1))

    near = [(i, i ^ 1) for i in range(tensor)]
    pair = [(i, i ^ CORES) for i in range(tensor)]
    far = [(i, (last - i) ^ 1) for i in range(tensor)]
    held = both(cotangent, lax.ppermute(cotangent, "tensor", near), my_core == 0)
    held = both(held, lax.ppermute(held, "tensor", pair), my_x % 2 == 0)
    full_cotangent = both(held, lax.ppermute(held, "tensor", far), my_x < 2)

    live = (token_adapter >= 0).astype(jnp.float32)

    pieces = pack(columns, block_adapter, owner_map, down_a.transpose(0, 2, 1), up_b)
    table = lax.all_to_all(
        pieces.reshape(dp, SPARE, LANES), "dp", 0, 0, axis_index_groups=plane
    )
    all_slots = table[:, own_slots, :block_count].astype(jnp.int32)
    table = table[:, :own_slots].reshape(dp * own_slots, LANES)

    onehot = (
        all_slots.reshape(-1, 1) == jnp.arange(dp * own_slots, dtype=jnp.int32)[None, :]
    ).astype(jnp.bfloat16)
    picked = jnp.dot(onehot, table, preferred_element_type=jnp.float32).astype(jnp.bfloat16)
    picked = lax.all_to_all(
        picked.reshape(dp, block_count, LANES), "dp", 0, 0, axis_index_groups=plane
    )
    picked = picked.reshape(chunks + 1, rank, block_count, LANES)
    down_sel = picked[:chunks].transpose(2, 1, 0, 3).reshape(block_count, rank, dpiece)
    up_sel = picked[chunks].transpose(1, 0, 2)

    input_blocks = inputs.reshape(block_count, blk_rows, dpiece)
    g_blocks = cotangent.reshape(block_count, blk_rows, kpiece)
    low_part = jnp.einsum("brd,bnd->brn", down_sel, input_blocks, preferred_element_type=jnp.float32)
    hid_part = jnp.einsum("brk,bnk->brn", up_sel, g_blocks, preferred_element_type=jnp.float32)
    part = jnp.concatenate([low_part, hid_part], axis=1).astype(jnp.bfloat16)
    part = lax.all_to_all(
        jnp.broadcast_to(part, (tensor,) + part.shape), "tensor", 0, 0, axis_index_groups=t_group
    )
    total = jnp.sum(part.astype(jnp.float32), axis=0) * live.reshape(block_count, 1, blk_rows)
    total = total.astype(jnp.bfloat16)
    low_rank, hidden = total[:, :rank], total[:, rank:]

    terms = adapter_scale_factor * jnp.einsum(
        "brn,bno->bro", low_rank, g_blocks, preferred_element_type=jnp.float32
    )
    terms = terms.astype(jnp.bfloat16)
    terms = lax.all_to_all(
        jnp.broadcast_to(terms, (LINE,) + terms.shape), "dp", 0, 0, axis_index_groups=y_groups
    )
    terms = terms.reshape(LINE * block_count, rank, kpiece)
    row_slots = lax.dynamic_slice_in_dim(all_slots, my_row * LINE, LINE, 0).reshape(-1)
    column_slots = (
        jnp.array([z_list.index(z) for z in last_list], jnp.int32)[:, None] * (LINE * own_slots)
        + my_y * own_slots
        + jnp.arange(own_slots, dtype=jnp.int32)[None, :]
    ).reshape(-1)
    owner_match = (column_slots[:, None] == row_slots[None, :]).astype(jnp.bfloat16)
    sums = jnp.einsum("sb,bro->sro", owner_match, terms, preferred_element_type=jnp.float32)
    sums = lax.all_to_all(
        sums.astype(jnp.bfloat16).reshape(columns, own_slots, rank, kpiece), "dp", 0, 0, axis_index_groups=z_groups
    )
    grad_b = jnp.sum(sums.astype(jnp.float32), axis=0)

    frozen = lax.dot_general(
        full_cotangent, base_weight, (((1,), (1,)), ((), ())), preferred_element_type=jnp.float32
    )
    adapter = jnp.einsum(
        "brn,brd->bnd", hidden, down_sel, preferred_element_type=jnp.float32
    ).reshape(row_count, dpiece)
    gradient = (frozen * live[:, None] + adapter_scale_factor * adapter).astype(jnp.bfloat16)
    return (gradient, grad_b)


def solution(mesh):
    in_specs = (
        P("dp", "tensor"),
        P("dp", "tensor"),
        P("tensor", None),
        P("dp", "tensor", None),
        P("dp", None, "tensor"),
        P("dp"),
        P("dp"),
        P(),
    )
    out_specs = (P("dp", "tensor"), P("dp", None, "tensor"))
    return jax.shard_map(
        on_device, mesh=mesh, in_specs=in_specs, out_specs=out_specs, check_vma=False
    )
```

```python
import functools

import jax
import jax.numpy as jnp
from jax import lax
from jax.experimental import pallas as pl
from jax.experimental.pallas import tpu as pltpu
from jax.sharding import PartitionSpec as P

adapter_scale_factor = 2.0
LINE = 8
FIRST_Z = 9
FIRST_Y = 4
LAST_Z = 7
FIRST_X = 2
LANES = 128
CORES = 2


SPARE = 4


def far_first(at, first, extent):
    past = lax.rem(at + (extent - first), extent) - extent // 2
    return lax.select(past >= 0, 2 * past + 1, lax.rem(-2 * past, extent))


def far_first_list(first, extent):
    aside = [first]
    for step in range(extent - 1):
        past = (step + 1) // 2
        past = past if step % 2 == 0 else -past
        aside.append((first + extent // 2 + past) % extent)
    return aside


def listed(z, y, columns):
    return far_first(z, FIRST_Z, columns), far_first(y, FIRST_Y, LINE)


def listed_slot(slot, slots, columns):
    owner = lax.div(slot, slots)
    z, y = listed(lax.div(owner, LINE), lax.rem(owner, LINE), columns)
    return (z * LINE + y) * slots + lax.rem(slot, slots)


def pack_kernel(columns, adapter_ref, owner_ref, down_ref, up_ref, out_ref):
    slots, rank, dpiece = down_ref.shape
    blocks = adapter_ref.shape[0]
    rows = rank * SPARE
    at = lax.broadcasted_iota(jnp.int32, (rows, slots * rank), 0)
    source = lax.broadcasted_iota(jnp.int32, (rows, slots * rank), 1)
    spread = (source == (at % SPARE) * rank + at // SPARE).astype(jnp.bfloat16)
    kind = lax.broadcasted_iota(jnp.int32, (rows, LANES), 0) % SPARE
    lane = lax.broadcasted_iota(jnp.int32, (rows, LANES), 1)
    numbers = jnp.zeros((rows, LANES), jnp.float32)
    for b in range(blocks):
        slot = listed_slot(owner_ref[adapter_ref[b]], slots, columns).astype(jnp.float32)
        numbers = jnp.where((kind == slots) & (lane == b), slot, numbers)
    down = jnp.concatenate([down_ref[j] for j in range(slots)], axis=0)
    up = jnp.concatenate([up_ref[j] for j in range(slots)], axis=0)
    for c in range(dpiece // LANES + 1):
        chunk = up if c == dpiece // LANES else down[:, c * LANES : (c + 1) * LANES]
        mixed = jnp.dot(spread, chunk, preferred_element_type=jnp.float32)
        out_ref[c * rows : (c + 1) * rows, :] = (mixed + numbers).astype(jnp.bfloat16)


def pack(columns, block_adapter, owner_map, down_rows, up_b):
    _, rank, dpiece = down_rows.shape
    smem = pl.BlockSpec(memory_space=pltpu.SMEM)
    vmem = pl.BlockSpec(memory_space=pltpu.VMEM)
    return pl.pallas_call(
        functools.partial(pack_kernel, columns),
        out_shape=jax.ShapeDtypeStruct((SPARE * rank * (dpiece // LANES + 1), LANES), jnp.bfloat16),
        in_specs=[smem, smem, vmem, vmem],
        out_specs=vmem,
    )(block_adapter, owner_map, down_rows, up_b)


def on_device(
    inputs, cotangent, base_weight, down_a, up_b, block_adapter, token_adapter, owner_map
):
    row_count, dpiece = inputs.shape
    kpiece = cotangent.shape[1]
    block_count = block_adapter.shape[0]
    blk_rows = row_count // block_count
    own_slots, _, rank = down_a.shape
    dp = lax.axis_size("dp")
    tensor = lax.axis_size("tensor")
    columns = dp // LINE
    chunks = dpiece // LANES
    z_list = far_first_list(FIRST_Z, columns)
    y_list = far_first_list(FIRST_Y, LINE)
    plane = [[z * LINE + y for z in z_list for y in y_list]]
    y_groups = [[z * LINE + y for y in y_list] for z in range(columns)]
    last_list = far_first_list(LAST_Z, columns)
    z_groups = [[z * LINE + y for z in last_list] for y in range(LINE)]
    x_list = far_first_list(FIRST_X, tensor // CORES)
    t_group = [[x * CORES + core for x in x_list for core in reversed(range(CORES))]]
    my_dp = lax.axis_index("dp")
    my_row, my_y = listed(lax.div(my_dp, LINE), lax.rem(my_dp, LINE), columns)

    my_tensor = lax.axis_index("tensor")
    my_x, my_core = my_tensor // CORES, my_tensor % CORES
    last = tensor - 1

    def both(mine, other, mine_first):
        return jnp.where(mine_first, jnp.concatenate([mine, other], axis=1), jnp.concatenate([other, mine], axis=1))

    near = [(i, i ^ 1) for i in range(tensor)]
    pair = [(i, i ^ CORES) for i in range(tensor)]
    far = [(i, (last - i) ^ 1) for i in range(tensor)]
    held = both(cotangent, lax.ppermute(cotangent, "tensor", near), my_core == 0)
    held = both(held, lax.ppermute(held, "tensor", pair), my_x % 2 == 0)
    swapped = lax.ppermute(held, "tensor", far)

    live = (token_adapter >= 0).astype(jnp.float32)

    pieces = pack(columns, block_adapter, owner_map, down_a.transpose(0, 2, 1), up_b)
    table = lax.all_to_all(
        pieces.reshape(dp, SPARE, LANES), "dp", 0, 0, axis_index_groups=plane
    )
    all_slots = table[:, own_slots, :block_count].astype(jnp.int32)
    table = table[:, :own_slots].reshape(dp * own_slots, LANES)

    onehot = (
        all_slots.reshape(-1, 1) == jnp.arange(dp * own_slots, dtype=jnp.int32)[None, :]
    ).astype(jnp.bfloat16)
    picked = jnp.dot(onehot, table, preferred_element_type=jnp.float32).astype(jnp.bfloat16)
    picked, late_weight = lax.optimization_barrier((picked, base_weight))
    low_weight, high_weight = jnp.split(late_weight, 2, axis=1)
    held_weight = jnp.where(my_x < 2, low_weight, high_weight)
    swapped_weight = jnp.where(my_x < 2, high_weight, low_weight)
    held_weight, swapped_weight = lax.optimization_barrier((held_weight, swapped_weight))
    picked = lax.all_to_all(
        picked.reshape(dp, block_count, LANES), "dp", 0, 0, axis_index_groups=plane
    )
    picked = picked.reshape(chunks + 1, rank, block_count, LANES)
    down_sel = picked[:chunks].transpose(2, 1, 0, 3).reshape(block_count, rank, dpiece)
    up_sel = picked[chunks].transpose(1, 0, 2)

    input_blocks = inputs.reshape(block_count, blk_rows, dpiece)
    g_blocks = cotangent.reshape(block_count, blk_rows, kpiece)
    low_part = jnp.einsum("brd,bnd->brn", down_sel, input_blocks, preferred_element_type=jnp.float32)
    hid_part = jnp.einsum("brk,bnk->brn", up_sel, g_blocks, preferred_element_type=jnp.float32)
    part = jnp.concatenate([low_part, hid_part], axis=1).astype(jnp.bfloat16)
    part = lax.all_to_all(
        jnp.broadcast_to(part, (tensor,) + part.shape), "tensor", 0, 0, axis_index_groups=t_group
    )
    total = jnp.sum(part.astype(jnp.float32), axis=0) * live.reshape(block_count, 1, blk_rows)
    total = total.astype(jnp.bfloat16)
    low_rank, hidden = total[:, :rank], total[:, rank:]

    terms = adapter_scale_factor * jnp.einsum(
        "brn,bno->bro", low_rank, g_blocks, preferred_element_type=jnp.float32
    )
    terms = terms.astype(jnp.bfloat16)
    terms, hidden = lax.optimization_barrier((terms, hidden))
    terms = lax.all_to_all(
        jnp.broadcast_to(terms, (LINE,) + terms.shape), "dp", 0, 0, axis_index_groups=y_groups
    )
    terms = terms.reshape(LINE * block_count, rank, kpiece)
    row_slots = lax.dynamic_slice_in_dim(all_slots, my_row * LINE, LINE, 0).reshape(-1)
    column_slots = (
        jnp.array([z_list.index(z) for z in last_list], jnp.int32)[:, None] * (LINE * own_slots)
        + my_y * own_slots
        + jnp.arange(own_slots, dtype=jnp.int32)[None, :]
    ).reshape(-1)
    owner_match = (column_slots[:, None] == row_slots[None, :]).astype(jnp.bfloat16)
    sums = jnp.einsum("sb,bro->sro", owner_match, terms, preferred_element_type=jnp.float32)
    sums = lax.all_to_all(
        sums.astype(jnp.bfloat16).reshape(columns, own_slots, rank, kpiece), "dp", 0, 0, axis_index_groups=z_groups
    )
    grad_b = jnp.sum(sums.astype(jnp.float32), axis=0)

    contract_last = (((1,), (1,)), ((), ()))
    adapter = jnp.einsum(
        "brn,brd->bnd", hidden, down_sel, preferred_element_type=jnp.float32
    ).reshape(row_count, dpiece)
    frozen = lax.dot_general(held, held_weight, contract_last, preferred_element_type=jnp.float32)
    early = lax.optimization_barrier(frozen * live[:, None] + adapter_scale_factor * adapter)
    frozen = lax.dot_general(
        swapped, swapped_weight, contract_last, preferred_element_type=jnp.float32
    )
    gradient = (early + frozen * live[:, None]).astype(jnp.bfloat16)
    return (gradient, grad_b)


def solution(mesh):
    in_specs = (
        P("dp", "tensor"),
        P("dp", "tensor"),
        P("tensor", None),
        P("dp", "tensor", None),
        P("dp", None, "tensor"),
        P("dp"),
        P("dp"),
        P(),
    )
    out_specs = (P("dp", "tensor"), P("dp", None, "tensor"))
    return jax.shard_map(
        on_device, mesh=mesh, in_specs=in_specs, out_specs=out_specs, check_vma=False
    )
```

```python
import functools

import jax
import jax.numpy as jnp
from jax import lax
from jax.experimental import pallas as pl
from jax.experimental.pallas import tpu as pltpu
from jax.sharding import PartitionSpec as P

adapter_scale_factor = 2.0
LINE = 8
FIRST_Z = 9
FIRST_Y = 4
LAST_Z = 6
FIRST_X = 2
LANES = 128
CORES = 2


SPARE = 4


def far_first(at, first, extent):
    past = lax.rem(at + (extent - first), extent) - extent // 2
    return lax.select(past >= 0, 2 * past + 1, lax.rem(-2 * past, extent))


def far_first_list(first, extent):
    aside = [first]
    for step in range(extent - 1):
        past = (step + 1) // 2
        past = past if step % 2 == 0 else -past
        aside.append((first + extent // 2 + past) % extent)
    return aside


def listed(z, y, columns):
    return far_first(z, FIRST_Z, columns), far_first(y, FIRST_Y, LINE)


def listed_slot(slot, slots, columns):
    owner = lax.div(slot, slots)
    z, y = listed(lax.div(owner, LINE), lax.rem(owner, LINE), columns)
    return (z * LINE + y) * slots + lax.rem(slot, slots)


def pack_kernel(columns, adapter_ref, owner_ref, down_ref, up_ref, out_ref):
    slots, rank, dpiece = down_ref.shape
    blocks = adapter_ref.shape[0]
    rows = rank * SPARE
    at = lax.broadcasted_iota(jnp.int32, (rows, slots * rank), 0)
    source = lax.broadcasted_iota(jnp.int32, (rows, slots * rank), 1)
    spread = (source == (at % SPARE) * rank + at // SPARE).astype(jnp.bfloat16)
    kind = lax.broadcasted_iota(jnp.int32, (rows, LANES), 0) % SPARE
    lane = lax.broadcasted_iota(jnp.int32, (rows, LANES), 1)
    numbers = jnp.zeros((rows, LANES), jnp.float32)
    for b in range(blocks):
        slot = listed_slot(owner_ref[adapter_ref[b]], slots, columns).astype(jnp.float32)
        numbers = jnp.where((kind == slots) & (lane == b), slot, numbers)
    down = jnp.concatenate([down_ref[j] for j in range(slots)], axis=0)
    up = jnp.concatenate([up_ref[j] for j in range(slots)], axis=0)
    for c in range(dpiece // LANES + 1):
        chunk = up if c == dpiece // LANES else down[:, c * LANES : (c + 1) * LANES]
        mixed = jnp.dot(spread, chunk, preferred_element_type=jnp.float32)
        out_ref[c * rows : (c + 1) * rows, :] = (mixed + numbers).astype(jnp.bfloat16)


def pack(columns, block_adapter, owner_map, down_rows, up_b):
    _, rank, dpiece = down_rows.shape
    smem = pl.BlockSpec(memory_space=pltpu.SMEM)
    vmem = pl.BlockSpec(memory_space=pltpu.VMEM)
    return pl.pallas_call(
        functools.partial(pack_kernel, columns),
        out_shape=jax.ShapeDtypeStruct((SPARE * rank * (dpiece // LANES + 1), LANES), jnp.bfloat16),
        in_specs=[smem, smem, vmem, vmem],
        out_specs=vmem,
    )(block_adapter, owner_map, down_rows, up_b)


def on_device(
    inputs, cotangent, base_weight, down_a, up_b, block_adapter, token_adapter, owner_map
):
    row_count, dpiece = inputs.shape
    kpiece = cotangent.shape[1]
    block_count = block_adapter.shape[0]
    blk_rows = row_count // block_count
    own_slots, _, rank = down_a.shape
    dp = lax.axis_size("dp")
    tensor = lax.axis_size("tensor")
    columns = dp // LINE
    chunks = dpiece // LANES
    z_list = far_first_list(FIRST_Z, columns)
    y_list = far_first_list(FIRST_Y, LINE)
    plane = [[z * LINE + y for z in z_list for y in y_list]]
    y_groups = [[z * LINE + y for y in y_list] for z in range(columns)]
    last_list = far_first_list(LAST_Z, columns)
    z_groups = [[z * LINE + y for z in last_list] for y in range(LINE)]
    x_list = far_first_list(FIRST_X, tensor // CORES)
    t_group = [[x * CORES + core for x in x_list for core in reversed(range(CORES))]]
    my_dp = lax.axis_index("dp")
    my_row, my_y = listed(lax.div(my_dp, LINE), lax.rem(my_dp, LINE), columns)

    my_tensor = lax.axis_index("tensor")
    my_x, my_core = my_tensor // CORES, my_tensor % CORES
    last = tensor - 1

    def both(mine, other, mine_first):
        return jnp.where(mine_first, jnp.concatenate([mine, other], axis=1), jnp.concatenate([other, mine], axis=1))

    near = [(i, i ^ 1) for i in range(tensor)]
    pair = [(i, i ^ CORES) for i in range(tensor)]
    far = [(i, (last - i) ^ 1) for i in range(tensor)]
    held = both(cotangent, lax.ppermute(cotangent, "tensor", near), my_core == 0)
    held = both(held, lax.ppermute(held, "tensor", pair), my_x % 2 == 0)
    swapped = lax.ppermute(held, "tensor", far)

    live = (token_adapter >= 0).astype(jnp.float32)

    pieces = pack(columns, block_adapter, owner_map, down_a.transpose(0, 2, 1), up_b)
    table = lax.all_to_all(
        pieces.reshape(dp, SPARE, LANES), "dp", 0, 0, axis_index_groups=plane
    )
    all_slots = table[:, own_slots, :block_count].astype(jnp.int32)
    table = table[:, :own_slots].reshape(dp * own_slots, LANES)

    onehot = (
        all_slots.reshape(-1, 1) == jnp.arange(dp * own_slots, dtype=jnp.int32)[None, :]
    ).astype(jnp.bfloat16)
    picked = jnp.dot(onehot, table, preferred_element_type=jnp.float32).astype(jnp.bfloat16)
    picked, late_weight = lax.optimization_barrier((picked, base_weight))
    low_weight, high_weight = jnp.split(late_weight, 2, axis=1)
    held_weight = jnp.where(my_x < 2, low_weight, high_weight)
    swapped_weight = jnp.where(my_x < 2, high_weight, low_weight)
    held_weight, swapped_weight = lax.optimization_barrier((held_weight, swapped_weight))
    picked = lax.all_to_all(
        picked.reshape(dp, block_count, LANES), "dp", 0, 0, axis_index_groups=plane
    )
    picked = picked.reshape(chunks + 1, rank, block_count, LANES)
    down_sel = picked[:chunks].transpose(2, 1, 0, 3).reshape(block_count, rank, dpiece)
    up_sel = picked[chunks].transpose(1, 0, 2)

    input_blocks = inputs.reshape(block_count, blk_rows, dpiece)
    g_blocks = cotangent.reshape(block_count, blk_rows, kpiece)
    low_part = jnp.einsum("brd,bnd->brn", down_sel, input_blocks, preferred_element_type=jnp.float32)
    hid_part = jnp.einsum("brk,bnk->brn", up_sel, g_blocks, preferred_element_type=jnp.float32)
    part = jnp.concatenate([low_part, hid_part], axis=1).astype(jnp.bfloat16)
    part = lax.all_to_all(
        jnp.broadcast_to(part, (tensor,) + part.shape), "tensor", 0, 0, axis_index_groups=t_group
    )
    total = jnp.sum(part.astype(jnp.float32), axis=0) * live.reshape(block_count, 1, blk_rows)
    total = total.astype(jnp.bfloat16)
    low_rank, hidden = total[:, :rank], total[:, rank:]

    terms = adapter_scale_factor * jnp.einsum(
        "brn,bno->bro", low_rank, g_blocks, preferred_element_type=jnp.float32
    )
    terms = terms.astype(jnp.bfloat16)
    terms, hidden = lax.optimization_barrier((terms, hidden))
    terms = lax.all_to_all(
        jnp.broadcast_to(terms, (LINE,) + terms.shape), "dp", 0, 0, axis_index_groups=y_groups
    )
    terms = terms.reshape(LINE * block_count, rank, kpiece)
    row_slots = lax.dynamic_slice_in_dim(all_slots, my_row * LINE, LINE, 0).reshape(-1)
    column_slots = (
        jnp.array([z_list.index(z) for z in last_list], jnp.int32)[:, None] * (LINE * own_slots)
        + my_y * own_slots
        + jnp.arange(own_slots, dtype=jnp.int32)[None, :]
    ).reshape(-1)
    owner_match = (column_slots[:, None] == row_slots[None, :]).astype(jnp.bfloat16)
    sums = jnp.einsum("sb,bro->sro", owner_match, terms, preferred_element_type=jnp.float32)
    sums = lax.all_to_all(
        sums.astype(jnp.bfloat16).reshape(columns, own_slots, rank, kpiece), "dp", 0, 0, axis_index_groups=z_groups
    )
    grad_b = jnp.sum(sums.astype(jnp.float32), axis=0)

    contract_last = (((1,), (1,)), ((), ()))
    adapter = jnp.einsum(
        "brn,brd->bnd", hidden, down_sel, preferred_element_type=jnp.float32
    ).reshape(row_count, dpiece)
    frozen = lax.dot_general(held, held_weight, contract_last, preferred_element_type=jnp.float32)
    early = lax.optimization_barrier(frozen * live[:, None] + adapter_scale_factor * adapter)
    frozen = lax.dot_general(
        swapped, swapped_weight, contract_last, preferred_element_type=jnp.float32
    )
    gradient = (early + frozen * live[:, None]).astype(jnp.bfloat16)
    return (gradient, grad_b)


def solution(mesh):
    in_specs = (
        P("dp", "tensor"),
        P("dp", "tensor"),
        P("tensor", None),
        P("dp", "tensor", None),
        P("dp", None, "tensor"),
        P("dp"),
        P("dp"),
        P(),
    )
    out_specs = (P("dp", "tensor"), P("dp", None, "tensor"))
    return jax.shard_map(
        on_device, mesh=mesh, in_specs=in_specs, out_specs=out_specs, check_vma=False
    )
```
